256 devices in a mesh: ka: 32 (over z_lo, x, core), an: 8 (over z_hi, y).
Axes of the slice: x: 4, y: 4, z: 8 (z_hi: 2, z_lo: 4; z = z_hi * 4 + z_lo), core: 2. Of those that a mesh axis runs over, the one named last changes fastest.
Arguments:
- out_grad: bfloat16 [1024, 12288], P('ka', 'an'), may hold values from -4 to 4
- saved_input: bfloat16 [1024, 49152], P('an', 'ka'), may hold values from -6 to 6
- down_weight: bfloat16 [49152, 12288], P('ka', 'an'), may hold values from -0.109375 to 0.109375
Outputs:
- weight_grad: bfloat16 [49152, 12288], P('ka', 'an')
- input_grad: bfloat16 [1024, 49152], P('an', 'ka')
The draws below stay inside these ranges and needn't reach their ends.
All inputs are finite; a program needn't handle non-finite values.
Results may differ from the reference program's by a relative error of at most 0.017.
Values may be sent and summed in bfloat16 or wider, within the bound.
No kernel may reach another device: no remote copies, remote signals or barrier semaphores. Data moves between devices by JAX's collectives and lax.ppermute only.
A program may use at most 64 MiB of HBM per device.

```python
import math
import jax
import jax.numpy as jnp
from jax import lax

D = 12288
FF = 49152
TOKENS = 1024
N_KA = 32
N_AN = 8


def levels(key, shape, pieces, smallest, high):
    level = 1.0
    for position, shards_of in pieces:
        draws = jax.random.uniform(jax.random.fold_in(jax.random.fold_in(key, 6), position), (shards_of,), jnp.float32, smallest / len(pieces), high / len(pieces))
        level = level * jnp.repeat(jnp.exp(draws), shape[position] // shards_of).reshape((-1,) + (1,) * (len(shape) - 1 - position))
    return level


def normal_values(key, shape, scale, reach, pieces=(), kind=jnp.bfloat16):
    factor_of = levels(key, shape, pieces, -0.22, 0.18) if pieces else 1.0
    entries = jax.random.normal(key, shape, jnp.float32) * scale * factor_of
    return jnp.minimum(jnp.maximum(entries, -reach), reach).astype(kind)


def setup_inputs(seed: int = 0) -> dict:
    streams_of = jax.random.split(jax.random.key(seed), 4)
    out_grad = normal_values(streams_of[0], (TOKENS, D), 0.3, 4.0, ((0, 32), (1, 8)))
    saved_input = normal_values(streams_of[1], (TOKENS, FF), 1.0, 6.0, ((0, 8), (1, 32)))
    down_weight = normal_values(streams_of[2], (FF, D), (D // 4) ** -0.5, 0.109375, ((0, 32), (1, 8)))
    return dict(out_grad=out_grad, saved_input=saved_input, down_weight=down_weight)


coef = math.sqrt(2.0 / math.pi)

def gelu_parts(x):
    u = coef * (x + 0.044715 * x * x * x)
    t = jnp.tanh(u)
    value = 0.5 * x * (1.0 + t)
    slope = 0.5 * (1.0 + t) + 0.5 * x * (1.0 - t * t) * coef * (1.0 + 3.0 * 0.044715 * x * x)
    return (value, slope)

def reference(out_grad, saved_input, down_weight):
    inputs = saved_input.astype(jnp.float32)
    value, slope = gelu_parts(inputs)
    activated = value.astype(jnp.bfloat16)
    block = FF // N_KA
    width = D // N_AN
    act_blocks = activated.reshape(TOKENS, N_KA, block).transpose(1, 0, 2)
    weight_blocks = down_weight.reshape(N_KA, block, D)
    grad_groups = out_grad.astype(jnp.float32).reshape(TOKENS, N_AN, width)

    def one_block(pair):
        act_piece, weight_piece = pair
        grad_w = lax.dot_general(act_piece, out_grad, (((0,), (0,)), ((), ())), preferred_element_type=jnp.float32)
        weight_groups = weight_piece.astype(jnp.float32).reshape(block, N_AN, width)
        partials = jnp.einsum('tgd,bgd->gtb', grad_groups, weight_groups)
        rounded = lax.optimization_barrier(partials.astype(jnp.bfloat16))
        grad_h = lax.optimization_barrier(jnp.sum(rounded.astype(jnp.float32), axis=0))
        return (grad_w.astype(jnp.bfloat16), grad_h)
    grad_ws, grad_hs = lax.map(one_block, (act_blocks, weight_blocks))
    weight_grad = grad_ws.reshape(FF, D)
    hidden_grad = grad_hs.transpose(1, 0, 2).reshape(TOKENS, FF)
    input_grad = (hidden_grad * slope).astype(jnp.bfloat16)
    return (weight_grad, input_grad)
```

```python
import math

import jax
import jax.numpy as jnp
from jax import lax
from jax.sharding import Mesh, PartitionSpec as P

coef = math.sqrt(2.0 / math.pi)
AXES = ("zl", "x", "c", "zh", "y")
SIZES = (4, 4, 2, 2, 4)
KA = ("zl", "x", "c")
AN = ("zh", "y")


def gelu_value(x):
    u = coef * (x + 0.044715 * x * x * x)
    return 0.5 * x * (1.0 + jnp.tanh(u))


def gelu_slope(x):
    t = jnp.tanh(coef * (x + 0.044715 * x * x * x))
    return 0.5 * (1.0 + t) + 0.5 * x * (1.0 - t * t) * coef * (1.0 + 3.0 * 0.044715 * x * x)


def send(v, axis, step):
    n = SIZES[AXES.index(axis)]
    return lax.ppermute(v, axis, [(i, (i + step) % n) for i in range(n)])


def place(blocks, me, n):
    out = jnp.zeros((n,) + blocks[0].shape, blocks[0].dtype)
    for k, b in enumerate(blocks):
        out = lax.dynamic_update_index_in_dim(out, b, lax.rem(me + (n - k), n), 0)
    return out


def body(out_grad, saved_input, weight):
    zl, x, c, zh, y = (lax.axis_index(a) for a in AXES)
    rows, width = out_grad.shape
    tok, hidden = saved_input.shape
    other = 1 - zh

    gz = place([out_grad] + [send(out_grad, "zl", k) for k in (1, 2, 3)], zl, 4)

    swapped = send(saved_input, "zh", 1)
    own = [saved_input] + [send(saved_input, "y", k) for k in (1, 2, 3)]
    far = [swapped] + [send(swapped, "y", k) for k in (1, 2, 3)]

    def finish(half):
        part = lax.dynamic_slice_in_dim(gz, 2 * half, 2, 0)
        gx = place([part] + [send(part, "x", k) for k in (1, 2, 3)], x, 4)
        both = place([gx, send(gx, "c", 1)], c, 2)
        return both.transpose(2, 1, 0, 3, 4).reshape(4 * tok, width)

    def partials(g):
        s = lax.dot_general(g, weight, (((1,), (1,)), ((), ())), preferred_element_type=jnp.float32)
        return s.astype(jnp.bfloat16).reshape(4, tok, hidden)

    def reduce_y(p):
        total = lax.dynamic_index_in_dim(p, y, 0, keepdims=False).astype(jnp.float32)
        for k in (1, 2, 3):
            b = lax.dynamic_index_in_dim(p, lax.rem(y + k, 4), 0, keepdims=False)
            total = total + send(b, "y", k).astype(jnp.float32)
        return total

    g_other = finish(other)
    r_other = send(reduce_y(partials(g_other)).astype(jnp.bfloat16), "zh", 1)
    g_mine = finish(zh)
    hidden_grad = reduce_y(partials(g_mine)) + r_other.astype(jnp.float32)
    input_grad = (hidden_grad * gelu_slope(saved_input.astype(jnp.float32))).astype(jnp.bfloat16)

    def act(blocks):
        out = jnp.zeros((4,) + blocks[0].shape, jnp.bfloat16)
        for k, b in enumerate(blocks):
            a = gelu_value(b.astype(jnp.float32)).astype(jnp.bfloat16)
            out = lax.dynamic_update_index_in_dim(out, a, lax.rem(y + (4 - k), 4), 0)
        return out.reshape(4 * tok, hidden)

    activated = jnp.concatenate([act(own), act(far)], 0)
    grads = jnp.concatenate([g_mine, g_other], 0)
    weight_grad = lax.dot_general(
        activated, grads, (((0,), (0,)), ((), ())), preferred_element_type=jnp.float32
    ).astype(jnp.bfloat16)
    return (weight_grad, input_grad)


def solution(mesh):
    fine = Mesh(mesh.devices.reshape(SIZES), AXES)
    return jax.shard_map(
        body,
        mesh=fine,
        in_specs=(P(KA, AN), P(AN, KA), P(KA, AN)),
        out_specs=(P(KA, AN), P(AN, KA)),
        check_vma=False,
    )
```

```python
import math

import jax
import jax.numpy as jnp
from jax import lax
from jax.sharding import Mesh, PartitionSpec as P

coef = math.sqrt(2.0 / math.pi)
AXES = ("zl", "x", "c", "zh", "y")
SIZES = (4, 4, 2, 2, 4)
KA = ("zl", "x", "c")
AN = ("zh", "y")


def gelu_value(x):
    u = coef * (x + 0.044715 * x * x * x)
    return 0.5 * x * (1.0 + jnp.tanh(u))


def gelu_slope(x):
    t = jnp.tanh(coef * (x + 0.044715 * x * x * x))
    return 0.5 * (1.0 + t) + 0.5 * x * (1.0 - t * t) * coef * (1.0 + 3.0 * 0.044715 * x * x)


def send(v, axis, step):
    n = SIZES[AXES.index(axis)]
    return lax.ppermute(v, axis, [(i, (i + step) % n) for i in range(n)])


def place(blocks, me, n):
    out = jnp.zeros((n,) + blocks[0].shape, blocks[0].dtype)
    for k, b in enumerate(blocks):
        out = lax.dynamic_update_index_in_dim(out, b, lax.rem(me + (n - k), n), 0)
    return out


def spread(v, axis, n):
    return lax.all_to_all(jnp.broadcast_to(v[None], (n,) + v.shape), axis, 0, 0, tiled=True)


def after(v, *done):
    return lax.optimization_barrier((v,) + done)[0]


def body(out_grad, saved_input, weight):
    zl, x, c, zh, y = (lax.axis_index(a) for a in AXES)
    rows, width = out_grad.shape
    tok, hidden = saved_input.shape

    def for_y(p, k):
        return lax.dynamic_index_in_dim(p, lax.rem(y + k, 4), 0, keepdims=False)

    def add_up(p, received):
        total = lax.dynamic_index_in_dim(p, y, 0, keepdims=False).astype(jnp.float32)
        for b in received:
            total = total + b.astype(jnp.float32)
        return total

    def act(blocks):
        out = jnp.zeros((4,) + blocks[0].shape, jnp.bfloat16)
        for k, b in enumerate(blocks):
            a = gelu_value(b.astype(jnp.float32)).astype(jnp.bfloat16)
            out = lax.dynamic_update_index_in_dim(out, a, lax.rem(y + (4 - k), 4), 0)
        return out.reshape(4 * tok, hidden)

    gz = place([out_grad] + [send(out_grad, "zl", k) for k in (1, 2, 3)], zl, 4)
    own1, own3 = (send(saved_input, "y", k) for k in (1, 3))

    gz = after(gz, own1, own3)
    gx = place([gz] + [send(gz, "x", k) for k in (1, 2, 3)], x, 4)
    swapped = send(after(saved_input, own1), "zh", 1)
    own2 = send(after(saved_input, own1), "y", 2)

    gc = place([gx, send(after(gx, swapped, own2), "c", 1)], c, 2)
    far1, far3 = (send(swapped, "y", k) for k in (1, 3))
    grads = gc.transpose(2, 1, 0, 3, 4).reshape(8 * tok, width)
    sums = lax.dot_general(grads, weight, (((1,), (1,)), ((), ())), preferred_element_type=jnp.float32)
    sums = sums.astype(jnp.bfloat16).reshape(2, 4, tok, hidden)
    p_other = lax.dynamic_index_in_dim(sums, 1 - zh, 0, keepdims=False)
    p_mine = lax.dynamic_index_in_dim(sums, zh, 0, keepdims=False)

    p_ready = after(p_other, far1, far3)
    r_other = [send(for_y(p_ready, k), "y", k) for k in (1, 3, 2)]
    far2 = send(after(swapped, far1), "y", 2)

    p_ready = after(p_mine, far2, r_other[0])
    r_mine = [send(for_y(p_ready, k), "y", k) for k in (1, 3, 2)]
    s_other = send(add_up(p_other, r_other).astype(jnp.bfloat16), "zh", 1)

    own = [after(b, gz) for b in (saved_input, own1, own2, own3)]
    far = [after(b, sums) for b in (swapped, far1, far2, far3)]
    low = lax.dynamic_update_index_in_dim(jnp.zeros((2, 4 * tok, hidden), jnp.bfloat16), act(own), zh, 0)
    activated = lax.dynamic_update_index_in_dim(low, act(far), 1 - zh, 0).reshape(8 * tok, hidden)
    weight_grad = lax.dot_general(
        activated, grads, (((0,), (0,)), ((), ())), preferred_element_type=jnp.float32
    ).astype(jnp.bfloat16)
    hidden_grad = add_up(p_mine, r_mine) + s_other.astype(jnp.float32)
    input_grad = (hidden_grad * gelu_slope(saved_input.astype(jnp.float32))).astype(jnp.bfloat16)
    return (weight_grad, input_grad)


def solution(mesh):
    fine = Mesh(mesh.devices.reshape(SIZES), AXES)
    return jax.shard_map(
        body,
        mesh=fine,
        in_specs=(P(KA, AN), P(AN, KA), P(KA, AN)),
        out_specs=(P(KA, AN), P(AN, KA)),
        check_vma=False,
    )
```

```python
import math

import jax
import jax.numpy as jnp
from jax import lax
from jax.sharding import Mesh, PartitionSpec as P

coef = math.sqrt(2.0 / math.pi)
AXES = ("zl", "x", "c", "zh", "y")
SIZES = (4, 4, 2, 2, 4)
KA = ("zl", "x", "c")
AN = ("zh", "y")


def gelu_value(x):
    u = coef * (x + 0.044715 * x * x * x)
    return 0.5 * x * (1.0 + jnp.tanh(u))


def gelu_slope(x):
    t = jnp.tanh(coef * (x + 0.044715 * x * x * x))
    return 0.5 * (1.0 + t) + 0.5 * x * (1.0 - t * t) * coef * (1.0 + 3.0 * 0.044715 * x * x)


def send(v, axis, step):
    n = SIZES[AXES.index(axis)]
    return lax.ppermute(v, axis, [(i, (i + step) % n) for i in range(n)])


def place(blocks, me, n):
    out = jnp.zeros((n,) + blocks[0].shape, blocks[0].dtype)
    for k, b in enumerate(blocks):
        out = lax.dynamic_update_index_in_dim(out, b, lax.rem(me + (n - k), n), 0)
    return out


def spread(v, axis, n):
    return lax.all_to_all(jnp.broadcast_to(v[None], (n,) + v.shape), axis, 0, 0, tiled=True)


def after(v, *done):
    return lax.optimization_barrier((v,) + done)[0]


def body(out_grad, saved_input, weight):
    zl, x, c, zh, y = (lax.axis_index(a) for a in AXES)
    rows, width = out_grad.shape
    tok, hidden = saved_input.shape

    def for_y(p, k):
        return lax.dynamic_index_in_dim(p, lax.rem(y + k, 4), 0, keepdims=False)

    def add_up(p, received):
        total = lax.dynamic_index_in_dim(p, y, 0, keepdims=False).astype(jnp.float32)
        for b in received:
            total = total + b.astype(jnp.float32)
        return total

    def act(blocks):
        out = jnp.zeros((4,) + blocks[0].shape, jnp.bfloat16)
        for k, b in enumerate(blocks):
            a = gelu_value(b.astype(jnp.float32)).astype(jnp.bfloat16)
            out = lax.dynamic_update_index_in_dim(out, a, lax.rem(y + (4 - k), 4), 0)
        return out.reshape(4 * tok, hidden)

    gz = place([out_grad] + [send(out_grad, "zl", k) for k in (1, 2, 3)], zl, 4)
    own1, own3 = (send(saved_input, "y", k) for k in (1, 3))

    gx1, gx3 = (send(gz, "x", k) for k in (1, 3))
    swapped = send(after(saved_input, gz), "zh", 1)
    gx2 = send(after(gz, own1), "x", 2)
    gx = place([gz, gx1, gx2, gx3], x, 4)
    own2 = send(after(saved_input, own3), "y", 2)

    gc = place([gx, send(after(gx, own1, own3), "c", 1)], c, 2)
    far1, far3, far2 = (send(swapped, "y", k) for k in (1, 3, 2))
    grads = gc.transpose(2, 1, 0, 3, 4).reshape(8 * tok, width)
    sums = lax.dot_general(grads, weight, (((1,), (1,)), ((), ())), preferred_element_type=jnp.float32)
    sums = sums.astype(jnp.bfloat16).reshape(2, 4, tok, hidden)
    p_other = lax.dynamic_index_in_dim(sums, 1 - zh, 0, keepdims=False)
    p_mine = lax.dynamic_index_in_dim(sums, zh, 0, keepdims=False)

    p_ready = after(p_other, far1, far3, own2)
    r_other = [send(for_y(p_ready, k), "y", k) for k in (1, 3, 2)]

    p_ready = after(p_mine, far2)
    r_mine = [send(for_y(p_ready, k), "y", k) for k in (1, 3, 2)]
    s_other = send(add_up(p_other, r_other).astype(jnp.bfloat16), "zh", 1)

    own = [saved_input, own1, own2, own3]
    far = [after(b, sums) for b in (swapped, far1, far2, far3)]
    low = lax.dynamic_update_index_in_dim(jnp.zeros((2, 4 * tok, hidden), jnp.bfloat16), act(own), zh, 0)
    activated = lax.dynamic_update_index_in_dim(low, act(far), 1 - zh, 0).reshape(8 * tok, hidden)
    weight_grad = lax.dot_general(
        activated, grads, (((0,), (0,)), ((), ())), preferred_element_type=jnp.float32
    ).astype(jnp.bfloat16)
    hidden_grad = add_up(p_mine, r_mine) + s_other.astype(jnp.float32)
    input_grad = (hidden_grad * gelu_slope(saved_input.astype(jnp.float32))).astype(jnp.bfloat16)
    return (weight_grad, input_grad)


def solution(mesh):
    fine = Mesh(mesh.devices.reshape(SIZES), AXES)
    return jax.shard_map(
        body,
        mesh=fine,
        in_specs=(P(KA, AN), P(AN, KA), P(KA, AN)),
        out_specs=(P(KA, AN), P(AN, KA)),
        check_vma=False,
    )
```

```python
import math

import jax
import jax.numpy as jnp
from jax import lax
from jax.sharding import Mesh, PartitionSpec as P

coef = math.sqrt(2.0 / math.pi)
AXES = ("zl", "x", "c", "zh", "y")
SIZES = (4, 4, 2, 2, 4)
KA = ("zl", "x", "c")
AN = ("zh", "y")


def gelu_value(x):
    u = coef * (x + 0.044715 * x * x * x)
    return 0.5 * x * (1.0 + jnp.tanh(u))


def gelu_slope(x):
    t = jnp.tanh(coef * (x + 0.044715 * x * x * x))
    return 0.5 * (1.0 + t) + 0.5 * x * (1.0 - t * t) * coef * (1.0 + 3.0 * 0.044715 * x * x)


def send(v, axis, step):
    n = SIZES[AXES.index(axis)]
    return lax.ppermute(v, axis, [(i, (i + step) % n) for i in range(n)])


def place(blocks, me, n):
    out = jnp.zeros((n,) + blocks[0].shape, blocks[0].dtype)
    for k, b in enumerate(blocks):
        out = lax.dynamic_update_index_in_dim(out, b, lax.rem(me + (n - k), n), 0)
    return out


def spread(v, axis, n):
    return lax.all_to_all(jnp.broadcast_to(v[None], (n,) + v.shape), axis, 0, 0, tiled=True)


def after(v, *done):
    return lax.optimization_barrier((v,) + done)[0]


def body(out_grad, saved_input, weight):
    zl, x, c, zh, y = (lax.axis_index(a) for a in AXES)
    rows, width = out_grad.shape
    tok, hidden = saved_input.shape

    def for_y(p, k):
        return lax.dynamic_index_in_dim(p, lax.rem(y + k, 4), 0, keepdims=False)

    def add_up(p, received):
        total = lax.dynamic_index_in_dim(p, y, 0, keepdims=False).astype(jnp.float32)
        for b in received:
            total = total + b.astype(jnp.float32)
        return total

    def act(blocks):
        out = jnp.zeros((4,) + blocks[0].shape, jnp.bfloat16)
        for k, b in enumerate(blocks):
            a = gelu_value(b.astype(jnp.float32)).astype(jnp.bfloat16)
            out = lax.dynamic_update_index_in_dim(out, a, lax.rem(y + (4 - k), 4), 0)
        return out.reshape(4 * tok, hidden)

    gz = place([out_grad] + [send(out_grad, "zl", k) for k in (1, 2, 3)], zl, 4)
    own1, own3 = (send(saved_input, "y", k) for k in (1, 3))

    gx1, gx3 = (send(gz, "x", k) for k in (1, 3))
    swapped = send(after(saved_input, gz), "zh", 1)
    gx2 = send(after(gz, own1), "x", 2)
    gx = place([gz, gx1, gx2, gx3], x, 4)
    own2 = send(after(saved_input, own3), "y", 2)

    gc = place([gx, send(after(gx, own1, own3), "c", 1)], c, 2)
    turn = after(swapped, gc)
    far1, far3 = (send(turn, "y", k) for k in (1, 3))
    far2 = send(after(own2, gc, swapped), "zh", 1)
    grads = gc.transpose(2, 1, 0, 3, 4).reshape(8 * tok, width)
    sums = lax.dot_general(grads, weight, (((1,), (1,)), ((), ())), preferred_element_type=jnp.float32)
    sums = sums.astype(jnp.bfloat16).reshape(2, 4, tok, hidden)
    p_other = lax.dynamic_index_in_dim(sums, 1 - zh, 0, keepdims=False)
    p_mine = lax.dynamic_index_in_dim(sums, zh, 0, keepdims=False)

    p_ready = p_other
    r_other = [send(for_y(p_ready, k), "y", k) for k in (1, 3, 2)]

    p_ready = after(p_mine, far1, far3, far2, r_other[0])
    r_mine = [send(for_y(p_ready, k), "y", k) for k in (1, 3, 2)]
    s_other = send(add_up(p_other, r_other).astype(jnp.bfloat16), "zh", 1)

    own = [saved_input, own1, own2, own3]
    far = [after(b, sums) for b in (swapped, far1, far2, far3)]
    low = lax.dynamic_update_index_in_dim(jnp.zeros((2, 4 * tok, hidden), jnp.bfloat16), act(own), zh, 0)
    activated = lax.dynamic_update_index_in_dim(low, act(far), 1 - zh, 0).reshape(8 * tok, hidden)
    weight_grad = lax.dot_general(
        activated, grads, (((0,), (0,)), ((), ())), preferred_element_type=jnp.float32
    ).astype(jnp.bfloat16)
    hidden_grad = add_up(p_mine, r_mine) + s_other.astype(jnp.float32)
    input_grad = (hidden_grad * gelu_slope(saved_input.astype(jnp.float32))).astype(jnp.bfloat16)
    return (weight_grad, input_grad)


def solution(mesh):
    fine = Mesh(mesh.devices.reshape(SIZES), AXES)
    return jax.shard_map(
        body,
        mesh=fine,
        in_specs=(P(KA, AN), P(AN, KA), P(KA, AN)),
        out_specs=(P(KA, AN), P(AN, KA)),
        check_vma=False,
    )
```

```python
import math

import jax
import jax.numpy as jnp
from jax import lax
from jax.sharding import Mesh, PartitionSpec as P

coef = math.sqrt(2.0 / math.pi)
AXES = ("zl", "x", "c", "zh", "y")
SIZES = (4, 4, 2, 2, 4)
KA = ("zl", "x", "c")
AN = ("zh", "y")


def gelu_value(x):
    u = coef * (x + 0.044715 * x * x * x)
    return 0.5 * x * (1.0 + jnp.tanh(u))


def gelu_slope(x):
    t = jnp.tanh(coef * (x + 0.044715 * x * x * x))
    return 0.5 * (1.0 + t) + 0.5 * x * (1.0 - t * t) * coef * (1.0 + 3.0 * 0.044715 * x * x)


def send(v, axis, step):
    n = SIZES[AXES.index(axis)]
    return lax.ppermute(v, axis, [(i, (i + step) % n) for i in range(n)])


def place(blocks, me, n):
    out = jnp.zeros((n,) + blocks[0].shape, blocks[0].dtype)
    for k, b in enumerate(blocks):
        out = lax.dynamic_update_index_in_dim(out, b, lax.rem(me + (n - k), n), 0)
    return out


def spread(v, axis, n):
    return lax.all_to_all(jnp.broadcast_to(v[None], (n,) + v.shape), axis, 0, 0, tiled=True)


def after(v, *done):
    return lax.optimization_barrier((v,) + done)[0]


def body(out_grad, saved_input, weight):
    zl, x, c, zh, y = (lax.axis_index(a) for a in AXES)
    rows, width = out_grad.shape
    tok, hidden = saved_input.shape

    def for_y(p, k):
        return lax.dynamic_index_in_dim(p, lax.rem(y + k, 4), 0, keepdims=False)

    def add_up(p, received):
        total = lax.dynamic_index_in_dim(p, y, 0, keepdims=False).astype(jnp.float32)
        for b in received:
            total = total + b.astype(jnp.float32)
        return total

    def act(blocks):
        out = jnp.zeros((4,) + blocks[0].shape, jnp.bfloat16)
        for k, b in enumerate(blocks):
            a = gelu_value(b.astype(jnp.float32)).astype(jnp.bfloat16)
            out = lax.dynamic_update_index_in_dim(out, a, lax.rem(y + (4 - k), 4), 0)
        return out.reshape(4 * tok, hidden)

    gz = place([out_grad] + [send(out_grad, "zl", k) for k in (1, 2, 3)], zl, 4)
    own1, own3 = (send(saved_input, "y", k) for k in (1, 3))

    gx1, gx3 = (send(gz, "x", k) for k in (1, 3))
    swapped = send(after(saved_input, gz), "zh", 1)
    gx2 = send(after(gz, own1), "x", 2)
    gx = place([gz, gx1, gx2, gx3], x, 4)
    own2 = send(after(saved_input, own3), "y", 2)

    gc = place([gx, send(after(gx, own1, own3), "c", 1)], c, 2)
    turn = after(swapped, gc)
    far1 = send(turn, "y", 1)
    far2 = send(after(own2, gc, swapped), "zh", 1)
    grads = gc.transpose(2, 1, 0, 3, 4).reshape(8 * tok, width)
    sums = lax.dot_general(grads, weight, (((1,), (1,)), ((), ())), preferred_element_type=jnp.float32)
    sums = sums.astype(jnp.bfloat16).reshape(2, 4, tok, hidden)
    p_other = lax.dynamic_index_in_dim(sums, 1 - zh, 0, keepdims=False)
    p_mine = lax.dynamic_index_in_dim(sums, zh, 0, keepdims=False)

    p_ready = p_other
    r_other = [send(for_y(p_ready, k), "y", k) for k in (1, 3, 2)]

    far3 = send(after(swapped, r_other[0]), "y", 3)
    p_ready = after(p_mine, far1, far2, r_other[0])
    r_mine = [send(for_y(p_ready, k), "y", k) for k in (1, 3, 2)]
    s_other = send(add_up(p_other, r_other).astype(jnp.bfloat16), "zh", 1)

    own = [saved_input, own1, own2, own3]
    far = [after(b, sums) for b in (swapped, far1, far2, far3)]
    low = lax.dynamic_update_index_in_dim(jnp.zeros((2, 4 * tok, hidden), jnp.bfloat16), act(own), zh, 0)
    activated = lax.dynamic_update_index_in_dim(low, act(far), 1 - zh, 0).reshape(8 * tok, hidden)
    weight_grad = lax.dot_general(
        activated, grads, (((0,), (0,)), ((), ())), preferred_element_type=jnp.float32
    ).astype(jnp.bfloat16)
    hidden_grad = add_up(p_mine, r_mine) + s_other.astype(jnp.float32)
    input_grad = (hidden_grad * gelu_slope(saved_input.astype(jnp.float32))).astype(jnp.bfloat16)
    return (weight_grad, input_grad)


def solution(mesh):
    fine = Mesh(mesh.devices.reshape(SIZES), AXES)
    return jax.shard_map(
        body,
        mesh=fine,
        in_specs=(P(KA, AN), P(AN, KA), P(KA, AN)),
        out_specs=(P(KA, AN), P(AN, KA)),
        check_vma=False,
    )
```
